32 devices in a mesh: groups: 2 (over y), ep: 8 (over z, x), tp: 2 (over core).
Axes of the slice: x: 2, y: 2, z: 4, core: 2. Of those that a mesh axis runs over, the one named last changes fastest.
Arguments:
- hidden: bfloat16 [64, 3584], P(('groups', 'ep')), parts along dimension 0, may hold values from -6 to 6
- expert_ids: int32 [64, 2], P(('groups', 'ep')), parts along dimension 0, may hold values from 0 to 1, all different within a row; in each aligned block of 4 rows (0 to 3, 4 to 7, ...) at most 4 rows name the same one
- gate_scores: float32 [64, 2], P(('groups', 'ep')), parts along dimension 0, may hold values from 0.05 to 1
- w_gate: bfloat16 [8, 896, 1024], P('ep', None, 'tp'), may hold values from -0.09375 to 0.09375
- w_up: bfloat16 [8, 896, 1024], P('ep', None, 'tp'), may hold values from -0.09375 to 0.09375
- w_down: bfloat16 [8, 1024, 896], P('ep', 'tp'), may hold values from -0.1875 to 0.1875
Outputs:
- combined: bfloat16 [64, 3584], P(('groups', 'ep')), parts along dimension 0
The draws below stay inside these ranges and needn't reach their ends.
There are 2 independent parts, one for each index of `groups`. The reference program is written for one: setup_inputs(seed, part) draws one part's arguments, and reference() takes and returns one part's arrays. A program takes and returns all parts, laid end to end along the dimension named above; an argument that names none is the same for every part. Nothing has to cross between parts.
Inputs may be any that keep to these rules, and one draw needn't show every extreme that they name: `expert_ids`: each row names 2 different experts. Within the rows of one device (aligned blocks of 4 tokens) no expert is named by more than 4 rows, a bound that some block reaches. Every expert is named somewhere.
All inputs are finite; a program needn't handle non-finite values.
Results may differ from the reference program's by a relative error of at most 0.0064.
Values may be sent and summed in bfloat16 or wider, within the bound.
No kernel may reach another device: no remote copies, remote signals or barrier semaphores. Data moves between devices by JAX's collectives and lax.ppermute only.
A program may use at most 64 MiB of HBM per device.

```python
import math
import jax
import jax.numpy as jnp
import numpy as np
from jax import lax

D = 3584
FF = 1024
GROUP = 4
TOK_DEV = 4
EXPERTS = 2
TOP = 2
CAP = 4
TOKENS = 32
N_EP = 8


def block_scale(stream_key, shape, cuts, least, largest):
    loudness = 1.0
    for position, blocks in cuts:
        heights = jax.random.uniform(jax.random.fold_in(jax.random.fold_in(stream_key, 6), position), (blocks,), jnp.float32, least / len(cuts), largest / len(cuts))
        loudness = loudness * jnp.repeat(jnp.exp(heights), shape[position] // blocks).reshape((-1,) + (1,) * (len(shape) - 1 - position))
    return loudness


def shared_out(own_key, own, number, rows, number_of, top, most, lean):
    order = jax.random.permutation(own_key, number_of)
    heavy_load, common = portions_of(number_of, rows * top, most, lean, True), portions_of(number_of, rows * top, most, lean, False)
    places = jnp.arange(number_of)

    def named(tallies, offset_by):
        used = int((tallies > 0).sum())
        fixed = max(1, used // 4)
        passed = fixed + (places - fixed + offset_by * (used - fixed)) % max(1, number_of - fixed)
        return jnp.zeros((number_of,), jnp.int32).at[order[jnp.where(places < fixed, places, passed)]].set(jnp.asarray(tallies, jnp.int32))

    tallies = jnp.where(number % 4 == 0, named(heavy_load, number // 4), named(common, number - number // 4 - 1))
    mixed = jax.random.permutation(jax.random.fold_in(own, 3), number_of)
    donor, receiver = mixed[0:number_of // 2 * 2:2], mixed[1:number_of // 2 * 2:2]
    slack = jnp.minimum(tallies[donor] - 1, most - tallies[receiver]) // 2
    slack = jnp.where((donor == order[0]) | (receiver == order[0]) | (tallies[receiver] == 0), 0, jnp.maximum(slack, 0))
    passed = jax.random.randint(jax.random.fold_in(own, 4), (number_of // 2,), 0, 1 << 20) % (slack + 1)
    tallies = tallies.at[donor].add(-passed).at[receiver].add(passed)
    labels = jnp.searchsorted(jnp.cumsum(tallies), jnp.arange(rows * top), side="right").astype(jnp.int32)
    listing = labels.reshape(top, rows).T
    listing = listing[jax.random.permutation(jax.random.fold_in(own, 1), rows)]
    offset_by = jax.random.randint(jax.random.fold_in(own, 2), (rows, 1), 0, top)
    return jnp.take_along_axis(listing, (jnp.arange(top)[None, :] + offset_by) % top, axis=1)


def portions_of(number_of, total, reach, skew, full):
    portions = [(1 << 20) // math.isqrt(standing ** skew) + 1 for standing in range(1, number_of + 1)]
    largest = reach if full else min(reach, max(-(-total // number_of), total * portions[0] // sum(portions)))
    least = 1 if total - largest >= number_of - 1 else 0
    counts, spare = [largest] + [least] * (number_of - 1), total - largest - least * (number_of - 1)
    while spare > 0:
        free = [i for i in range(1, number_of) if counts[i] < largest] or [i for i in range(1, number_of) if counts[i] < reach]
        pool, budget = sum([portions[i] for i in free]), spare
        for i in free:
            more = min(reach - counts[i], max(1, budget * portions[i] // pool), spare)
            counts[i] = counts[i] + more
            spare = spare - more
    return np.array(counts)


def normal_values(stream_key, shape, deviation, reach, cuts=(), kind=jnp.bfloat16):
    loudness = block_scale(stream_key, shape, cuts, -0.22, 0.18) if cuts else 1.0
    array = jax.random.normal(stream_key, shape, jnp.float32) * deviation * loudness
    return jnp.minimum(jnp.maximum(array, -reach), reach).astype(kind)


def setup_inputs(seed: int = 0, part: int = 0) -> dict:
    seeds = jax.random.split(jax.random.key(seed), 7)
    own_keys = jax.random.split(jax.random.fold_in(seeds[6], part), 7)
    hidden = normal_values(own_keys[0], (TOKENS, D), 1.0, 6.0, ((0, 8),))
    expert_ids_keys = jax.random.split(jax.random.fold_in(own_keys[1], 1), TOKENS // TOK_DEV)
    expert_ids_turns = jax.random.permutation(jax.random.fold_in(own_keys[1], 3), TOKENS // TOK_DEV)
    expert_ids = jax.vmap(lambda own, number: shared_out(jax.random.fold_in(own_keys[1], 2), own, number, TOK_DEV, EXPERTS, TOP, CAP, 2))(expert_ids_keys, expert_ids_turns).reshape((TOKENS, TOP))
    gate_scores = jnp.clip(jnp.exp(math.log(1.0) - 2.9957323 * jax.random.uniform(own_keys[2], (TOKENS, TOP), jnp.float32) ** block_scale(own_keys[2], (TOKENS, TOP), ((0, 8),), -0.2, 0.2)), 0.05, 1.0)
    w_gate = normal_values(seeds[3], (N_EP, D // GROUP, FF), D ** -0.5, 0.09375, ((0, 8), (2, 2)))
    w_up = normal_values(seeds[4], (N_EP, D // GROUP, FF), D ** -0.5, 0.09375, ((0, 8), (2, 2)))
    w_down = normal_values(seeds[5], (N_EP, FF, D // GROUP), FF ** -0.5, 0.1875, ((0, 8), (1, 2)))
    return {"hidden": hidden, "expert_ids": expert_ids, "gate_scores": gate_scores, "w_gate": w_gate, "w_up": w_up, "w_down": w_down}


route_scale = 2.5


def reference(hidden, expert_ids, gate_scores, w_gate, w_up, w_down):
    token_count, width_all = hidden.shape
    route_count = expert_ids.shape[1]
    experts = N_EP // GROUP
    slot_count = N_EP * CAP
    hidden_units = w_gate.shape[2]
    routing = (gate_scores / jnp.sum(gate_scores, axis=1, keepdims=True) * route_scale).astype(jnp.bfloat16)
    flat_ids = expert_ids.reshape(-1).astype(jnp.int32)
    expert_hot = (flat_ids[:, None] == jnp.arange(experts, dtype=jnp.int32)[None, :]).astype(jnp.int32)
    ranking = jnp.sum((jnp.cumsum(expert_hot, axis=0) - expert_hot) * expert_hot, axis=1).astype(jnp.int32)
    token_of = (jnp.arange(token_count * route_count, dtype=jnp.int32) // route_count).astype(jnp.int32)
    row_table = jnp.zeros((experts, slot_count), jnp.int32).at[flat_ids, ranking].set(token_of)
    row_share = jnp.zeros((experts, slot_count), jnp.float32).at[flat_ids, ranking].set(routing.reshape(-1).astype(jnp.float32))
    gate_all = w_gate.reshape(experts, width_all, hidden_units)
    up_all = w_up.reshape(experts, width_all, hidden_units)
    down_all = w_down.reshape(experts, GROUP, hidden_units, width_all // GROUP)

    def per_expert(totals, pieces):
        indices, shares, gate_weight, up_weight, down_parts = pieces
        rows_in = hidden[indices]
        gate_value = jnp.dot(rows_in, gate_weight, preferred_element_type=jnp.float32)
        up_value = jnp.dot(rows_in, up_weight, preferred_element_type=jnp.float32)
        inner_rows = (jax.nn.silu(gate_value) * up_value).astype(jnp.bfloat16)
        down_weight = jnp.transpose(down_parts, (1, 0, 2)).reshape(hidden_units, width_all)
        expert_out = jnp.dot(inner_rows, down_weight, preferred_element_type=jnp.float32).astype(jnp.bfloat16)
        totals = totals.at[indices].add(shares[:, None] * expert_out.astype(jnp.float32))
        return totals, None

    totals, unused = lax.scan(per_expert, jnp.zeros((token_count, width_all), jnp.float32),
                              (row_table, row_share, gate_all, up_all, down_all))
    return totals.astype(jnp.bfloat16)
```

```python
import jax
import jax.numpy as jnp
from jax import lax
from jax.sharding import PartitionSpec as P

GROUP = 4


route_scale = 2.5


def swapped(value, mask, crossed):
    ranks = lax.axis_size("ep")
    cores = lax.axis_size("tp")
    pairs = []
    for source in range(ranks):
        for core in range(cores):
            target_core = (core + 1) % cores if crossed else core
            pairs.append((source * cores + core, (source ^ mask) * cores + target_core))
    return lax.ppermute(value, ("ep", "tp"), pairs)


def ordered(own, other, bit):
    return jnp.stack([jnp.where(bit, other, own), jnp.where(bit, own, other)])


def spread_tokens(hidden):
    tok_rows, width_all = hidden.shape
    peers = lax.axis_size("ep")
    rank = lax.axis_index("ep")
    quarter = width_all // GROUP
    halves = GROUP
    block = hidden.reshape(tok_rows, GROUP, quarter).transpose(1, 0, 2)[:, None]
    mask = 1
    while mask < peers:
        bit = (rank & mask) > 0
        if halves > 1:
            parts = block.reshape((halves // 2, 2) + block.shape[1:])
            own = jnp.where(bit, parts[:, 1], parts[:, 0])
            sent = jnp.where(bit, parts[:, 0], parts[:, 1])
            halves //= 2
        else:
            own = sent = block
        other = swapped(sent, mask, True)
        both = ordered(own, other, bit)
        block = jnp.moveaxis(both, 0, 1).reshape(own.shape[0], 2 * own.shape[1], tok_rows, quarter)
        mask *= 2
    return block[0]


def route_tables(expert_ids, experts, capacity):
    tok_rows, route_count = expert_ids.shape
    flat_ids = expert_ids.reshape(-1)
    expert_hot = (flat_ids[:, None] == jnp.arange(experts, dtype=jnp.int32)[None, :]).astype(
        jnp.int32
    )
    ranking = jnp.sum((jnp.cumsum(expert_hot, axis=0) - expert_hot) * expert_hot, axis=1)
    slot_hot = (ranking[:, None] == jnp.arange(capacity, dtype=jnp.int32)[None, :]).astype(
        jnp.float32
    )
    expert_float = expert_hot.astype(jnp.float32).reshape(tok_rows, route_count, experts)
    return (expert_float, slot_hot.reshape(tok_rows, route_count, capacity))


def local(hidden, expert_ids, gate_scores, w_gate, w_up, w_down):
    tok_rows, width_all = hidden.shape
    route_count = expert_ids.shape[1]
    peer_count = lax.axis_size("ep")
    core_count = lax.axis_size("tp")
    experts = peer_count // GROUP
    quarter = width_all // GROUP
    group_bits = GROUP.bit_length() - 1
    every_expert = route_count == experts
    if every_expert:
        capacity = tok_rows
        arrived = spread_tokens(hidden)
    else:
        capacity = min(tok_rows, 2 * tok_rows * route_count // experts)
        expert_hot, slot_hot = route_tables(expert_ids, experts, capacity)
        placing = jnp.einsum("tke,tkc->ect", expert_hot, slot_hot).astype(jnp.bfloat16)
        outgoing = jnp.einsum(
            "ect,tgd->egcd",
            placing,
            hidden.reshape(tok_rows, GROUP, quarter),
            preferred_element_type=jnp.float32,
        ).astype(jnp.bfloat16)
        outgoing = outgoing.reshape(peer_count, capacity, quarter)
        arrived = lax.all_to_all(outgoing, "ep", split_axis=0, concat_axis=0, tiled=True)
    row_block = arrived.reshape(peer_count * capacity, quarter)
    gate_part = jnp.dot(row_block, w_gate[0], preferred_element_type=jnp.float32)
    up_part = jnp.dot(row_block, w_up[0], preferred_element_type=jnp.float32)
    parts = jnp.concatenate([gate_part, up_part], axis=1)
    for bit_index in range(group_bits):
        other = swapped(parts.astype(jnp.bfloat16), 2**bit_index, False)
        parts = parts + other.astype(jnp.float32)
    hidden_units = gate_part.shape[1]
    inner_rows = (jax.nn.silu(parts[:, :hidden_units]) * parts[:, hidden_units:]).astype(
        jnp.bfloat16
    )
    partial_out = jnp.dot(inner_rows, w_down[0], preferred_element_type=jnp.float32)
    partial_out = partial_out.astype(jnp.bfloat16).reshape(peer_count, 1, capacity, quarter)
    leaving = jnp.broadcast_to(partial_out, (peer_count, core_count, capacity, quarter))
    returned = lax.all_to_all(
        leaving.reshape(peer_count * core_count, capacity, quarter),
        ("ep", "tp"),
        split_axis=0,
        concat_axis=0,
        tiled=True,
    ).reshape(experts, GROUP, core_count, capacity, quarter)
    routing = (gate_scores / jnp.sum(gate_scores, axis=1, keepdims=True) * route_scale).astype(
        jnp.bfloat16
    )
    routing = routing.astype(jnp.float32)
    if every_expert:
        named = expert_ids[:, :, None] == jnp.arange(experts, dtype=jnp.int32)
        share = jnp.sum(jnp.where(named, routing[:, :, None], 0.0), axis=1)
        weighted = returned.astype(jnp.float32) * share.T[:, None, None, :, None]
        combined = jnp.sum(weighted, axis=(0, 2)).transpose(1, 0, 2)
    else:
        combining = jnp.einsum("tk,tke,tkc->tec", routing, expert_hot, slot_hot)
        combined = jnp.einsum(
            "tec,egpcd->tgd",
            combining.astype(jnp.bfloat16),
            returned,
            preferred_element_type=jnp.float32,
        )
    return combined.reshape(tok_rows, width_all).astype(jnp.bfloat16)


def solution(mesh):
    return jax.shard_map(
        local,
        mesh=mesh,
        in_specs=(
            P(("groups", "ep"), None),
            P(("groups", "ep"), None),
            P(("groups", "ep"), None),
            P("ep", None, "tp"),
            P("ep", None, "tp"),
            P("ep", "tp", None),
        ),
        out_specs=P(("groups", "ep"), None),
        check_vma=False,
    )
```

```python
import jax
import jax.numpy as jnp
from jax import lax
from jax.sharding import PartitionSpec as P

GROUP = 4


route_scale = 2.5


def swapped(value, mask, crossed):
    ranks = lax.axis_size("ep")
    cores = lax.axis_size("tp")
    pairs = []
    for source in range(ranks):
        for core in range(cores):
            target_core = (core + 1) % cores if crossed else core
            pairs.append((source * cores + core, (source ^ mask) * cores + target_core))
    return lax.ppermute(value, ("ep", "tp"), pairs)


def ordered(own, other, bit):
    return jnp.stack([jnp.where(bit, other, own), jnp.where(bit, own, other)])


def spread_tokens(hidden):
    tok_rows, width_all = hidden.shape
    peers = lax.axis_size("ep")
    rank = lax.axis_index("ep")
    quarter = width_all // GROUP
    halves = GROUP
    block = hidden.reshape(tok_rows, GROUP, quarter).transpose(1, 0, 2)[:, None]
    mask = 1
    while mask < peers:
        bit = (rank & mask) > 0
        if halves > 1:
            parts = block.reshape((halves // 2, 2) + block.shape[1:])
            own = jnp.where(bit, parts[:, 1], parts[:, 0])
            sent = jnp.where(bit, parts[:, 0], parts[:, 1])
            halves //= 2
        else:
            own = sent = block
        own, sent = lax.optimization_barrier((own, sent))
        other = swapped(sent, mask, True)
        both = ordered(own, other, bit)
        block = jnp.moveaxis(both, 0, 1).reshape(own.shape[0], 2 * own.shape[1], tok_rows, quarter)
        mask *= 2
    return block[0]


def route_tables(expert_ids, experts, capacity):
    tok_rows, route_count = expert_ids.shape
    flat_ids = expert_ids.reshape(-1)
    expert_hot = (flat_ids[:, None] == jnp.arange(experts, dtype=jnp.int32)[None, :]).astype(
        jnp.int32
    )
    ranking = jnp.sum((jnp.cumsum(expert_hot, axis=0) - expert_hot) * expert_hot, axis=1)
    slot_hot = (ranking[:, None] == jnp.arange(capacity, dtype=jnp.int32)[None, :]).astype(
        jnp.float32
    )
    expert_float = expert_hot.astype(jnp.float32).reshape(tok_rows, route_count, experts)
    return (expert_float, slot_hot.reshape(tok_rows, route_count, capacity))


def local(hidden, expert_ids, gate_scores, w_gate, w_up, w_down):
    tok_rows, width_all = hidden.shape
    route_count = expert_ids.shape[1]
    peer_count = lax.axis_size("ep")
    core_count = lax.axis_size("tp")
    experts = peer_count // GROUP
    quarter = width_all // GROUP
    group_bits = GROUP.bit_length() - 1
    every_expert = route_count == experts
    if every_expert:
        capacity = tok_rows
        arrived = spread_tokens(hidden)
    else:
        capacity = min(tok_rows, 2 * tok_rows * route_count // experts)
        expert_hot, slot_hot = route_tables(expert_ids, experts, capacity)
        placing = jnp.einsum("tke,tkc->ect", expert_hot, slot_hot).astype(jnp.bfloat16)
        outgoing = jnp.einsum(
            "ect,tgd->egcd",
            placing,
            hidden.reshape(tok_rows, GROUP, quarter),
            preferred_element_type=jnp.float32,
        ).astype(jnp.bfloat16)
        outgoing = outgoing.reshape(peer_count, capacity, quarter)
        arrived = lax.all_to_all(outgoing, "ep", split_axis=0, concat_axis=0, tiled=True)
    row_block = arrived.reshape(peer_count * capacity, quarter)
    weights_in = jnp.concatenate([w_gate[0], w_up[0]], axis=1)
    parts = jnp.dot(row_block, weights_in, preferred_element_type=jnp.float32)
    for bit_index in range(group_bits):
        other = swapped(parts.astype(jnp.bfloat16), 2**bit_index, False)
        parts = parts + other.astype(jnp.float32)
    hidden_units = w_gate.shape[2]
    inner_rows = (jax.nn.silu(parts[:, :hidden_units]) * parts[:, hidden_units:]).astype(
        jnp.bfloat16
    )
    partial_out = jnp.dot(inner_rows, w_down[0], preferred_element_type=jnp.float32)
    routing = (gate_scores / jnp.sum(gate_scores, axis=1, keepdims=True) * route_scale).astype(
        jnp.bfloat16
    )
    routing = routing.astype(jnp.float32)
    if every_expert:
        named = expert_ids[:, :, None] == jnp.arange(experts, dtype=jnp.int32)
        share = jnp.sum(jnp.where(named, routing[:, :, None], 0.0), axis=1)
    else:
        share = jnp.einsum("tk,tke,tkc->tec", routing, expert_hot, slot_hot).astype(jnp.bfloat16)
    partial_out = partial_out.astype(jnp.bfloat16).reshape(peer_count, 1, capacity, quarter)
    leaving = jnp.broadcast_to(partial_out, (peer_count, core_count, capacity, quarter))
    leaving, share = lax.optimization_barrier((leaving, share))
    returned = lax.all_to_all(
        leaving.reshape(peer_count * core_count, capacity, quarter),
        ("ep", "tp"),
        split_axis=0,
        concat_axis=0,
        tiled=True,
    ).reshape(experts, GROUP, core_count, capacity, quarter)
    if every_expert:
        weighted = returned.astype(jnp.float32) * share.T[:, None, None, :, None]
        combined = jnp.sum(weighted, axis=(0, 2)).transpose(1, 0, 2)
    else:
        combined = jnp.einsum(
            "tec,egpcd->tgd", share, returned, preferred_element_type=jnp.float32
        )
    return combined.reshape(tok_rows, width_all).astype(jnp.bfloat16)


def solution(mesh):
    return jax.shard_map(
        local,
        mesh=mesh,
        in_specs=(
            P(("groups", "ep"), None),
            P(("groups", "ep"), None),
            P(("groups", "ep"), None),
            P("ep", None, "tp"),
            P("ep", None, "tp"),
            P("ep", "tp", None),
        ),
        out_specs=P(("groups", "ep"), None),
        check_vma=False,
    )
```

```python
import jax
import jax.numpy as jnp
from jax import lax
from jax.sharding import PartitionSpec as P

GROUP = 4


route_scale = 2.5


def swapped(value, mask, crossed):
    ranks = lax.axis_size("ep")
    cores = lax.axis_size("tp")
    pairs = []
    for source in range(ranks):
        for core in range(cores):
            target_core = (core + 1) % cores if crossed else core
            pairs.append((source * cores + core, (source ^ mask) * cores + target_core))
    return lax.ppermute(value, ("ep", "tp"), pairs)


def ordered(own, other, bit):
    return jnp.stack([jnp.where(bit, other, own), jnp.where(bit, own, other)])


def spread_tokens(hidden):
    tok_rows, width_all = hidden.shape
    peers = lax.axis_size("ep")
    rank = lax.axis_index("ep")
    quarter = width_all // GROUP
    other = swapped(hidden, 1, True)
    bit = (rank & 1) > 0

    def kept(rows):
        quarters = rows.reshape(tok_rows, GROUP // 2, 2, quarter)
        return jnp.where(bit, quarters[:, :, 1], quarters[:, :, 0]).transpose(1, 0, 2)

    own = lax.optimization_barrier(kept(hidden))
    block = jnp.moveaxis(ordered(own, kept(other), bit), 0, 1)
    halves = GROUP // 2
    mask = 2
    while mask < peers:
        bit = (rank & mask) > 0
        if halves > 1:
            parts = block.reshape((halves // 2, 2) + block.shape[1:])
            own = jnp.where(bit, parts[:, 1], parts[:, 0])
            sent = jnp.where(bit, parts[:, 0], parts[:, 1])
            halves //= 2
        else:
            own = sent = block
        other = swapped(sent, mask, True)
        both = ordered(own, other, bit)
        block = jnp.moveaxis(both, 0, 1).reshape(own.shape[0], 2 * own.shape[1], tok_rows, quarter)
        mask *= 2
    return block[0]


def route_tables(expert_ids, experts, capacity):
    tok_rows, route_count = expert_ids.shape
    flat_ids = expert_ids.reshape(-1)
    expert_hot = (flat_ids[:, None] == jnp.arange(experts, dtype=jnp.int32)[None, :]).astype(
        jnp.int32
    )
    ranking = jnp.sum((jnp.cumsum(expert_hot, axis=0) - expert_hot) * expert_hot, axis=1)
    slot_hot = (ranking[:, None] == jnp.arange(capacity, dtype=jnp.int32)[None, :]).astype(
        jnp.float32
    )
    expert_float = expert_hot.astype(jnp.float32).reshape(tok_rows, route_count, experts)
    return (expert_float, slot_hot.reshape(tok_rows, route_count, capacity))


def local(hidden, expert_ids, gate_scores, w_gate, w_up, w_down):
    tok_rows, width_all = hidden.shape
    route_count = expert_ids.shape[1]
    peer_count = lax.axis_size("ep")
    core_count = lax.axis_size("tp")
    experts = peer_count // GROUP
    quarter = width_all // GROUP
    group_bits = GROUP.bit_length() - 1
    every_expert = route_count == experts
    if every_expert:
        capacity = tok_rows
        arrived = spread_tokens(hidden)
    else:
        capacity = min(tok_rows, 2 * tok_rows * route_count // experts)
        expert_hot, slot_hot = route_tables(expert_ids, experts, capacity)
        placing = jnp.einsum("tke,tkc->ect", expert_hot, slot_hot).astype(jnp.bfloat16)
        outgoing = jnp.einsum(
            "ect,tgd->egcd",
            placing,
            hidden.reshape(tok_rows, GROUP, quarter),
            preferred_element_type=jnp.float32,
        ).astype(jnp.bfloat16)
        outgoing = outgoing.reshape(peer_count, capacity, quarter)
        arrived = lax.all_to_all(outgoing, "ep", split_axis=0, concat_axis=0, tiled=True)
    row_block = arrived.reshape(peer_count * capacity, quarter)
    weights_in = lax.optimization_barrier(jnp.concatenate([w_gate[0], w_up[0]], axis=1))
    parts = jnp.dot(row_block, weights_in, preferred_element_type=jnp.float32)
    for bit_index in range(group_bits):
        other = swapped(parts.astype(jnp.bfloat16), 2**bit_index, False)
        parts = parts + other.astype(jnp.float32)
    hidden_units = w_gate.shape[2]
    inner_rows = (jax.nn.silu(parts[:, :hidden_units]) * parts[:, hidden_units:]).astype(
        jnp.bfloat16
    )
    partial_out = jnp.dot(inner_rows, w_down[0], preferred_element_type=jnp.float32)
    routing = (gate_scores / jnp.sum(gate_scores, axis=1, keepdims=True) * route_scale).astype(
        jnp.bfloat16
    )
    routing = routing.astype(jnp.float32)
    if every_expert:
        named = expert_ids[:, :, None] == jnp.arange(experts, dtype=jnp.int32)
        share = jnp.sum(jnp.where(named, routing[:, :, None], 0.0), axis=1)
    else:
        share = jnp.einsum("tk,tke,tkc->tec", routing, expert_hot, slot_hot).astype(jnp.bfloat16)
    partial_out = partial_out.astype(jnp.bfloat16).reshape(peer_count, 1, capacity, quarter)
    leaving = jnp.broadcast_to(partial_out, (peer_count, core_count, capacity, quarter))
    leaving, share = lax.optimization_barrier((leaving, share))
    returned = lax.all_to_all(
        leaving.reshape(peer_count * core_count, capacity, quarter),
        ("ep", "tp"),
        split_axis=0,
        concat_axis=0,
        tiled=True,
    ).reshape(experts, GROUP, core_count, capacity, quarter)
    if every_expert:
        weighted = returned.astype(jnp.float32) * share.T[:, None, None, :, None]
        combined = jnp.sum(weighted, axis=(0, 2)).transpose(1, 0, 2)
    else:
        combined = jnp.einsum(
            "tec,egpcd->tgd", share, returned, preferred_element_type=jnp.float32
        )
    return combined.reshape(tok_rows, width_all).astype(jnp.bfloat16)


def solution(mesh):
    return jax.shard_map(
        local,
        mesh=mesh,
        in_specs=(
            P(("groups", "ep"), None),
            P(("groups", "ep"), None),
            P(("groups", "ep"), None),
            P("ep", None, "tp"),
            P("ep", None, "tp"),
            P("ep", "tp", None),
        ),
        out_specs=P(("groups", "ep"), None),
        check_vma=False,
    )
```

```python
import jax
import jax.numpy as jnp
from jax import lax
from jax.sharding import PartitionSpec as P

GROUP = 4


route_scale = 2.5


def swapped(value, mask, crossed):
    ranks = lax.axis_size("ep")
    cores = lax.axis_size("tp")
    pairs = []
    for source in range(ranks):
        for core in range(cores):
            target_core = (core + 1) % cores if crossed else core
            pairs.append((source * cores + core, (source ^ mask) * cores + target_core))
    return lax.ppermute(value, ("ep", "tp"), pairs)


def core_sum(value):
    cores = lax.axis_size("tp")
    total = value
    for step in range(1, cores):
        pairs = [(core, (core + step) % cores) for core in range(cores)]
        total = total + lax.ppermute(value, "tp", pairs)
    return total


def by_xor(blocks, rank):
    mask = 1
    while mask < len(blocks):
        bit = (rank & mask) > 0
        blocks = [
            jnp.where(bit, blocks[index ^ mask], blocks[index]) for index in range(len(blocks))
        ]
        mask *= 2
    return blocks


def quarters_of(rows):
    quarter = rows.shape[1] // GROUP
    return [rows[:, index * quarter : (index + 1) * quarter] for index in range(GROUP)]


def spread_tokens(hidden):
    rank = lax.axis_index("ep")
    whole = {mask: swapped(hidden, mask, True) for mask in range(1, GROUP)}
    own = lax.optimization_barrier(by_xor(quarters_of(hidden), rank)[0])
    arrived = [own] + [by_xor(quarters_of(whole[mask]), rank)[0] for mask in range(1, GROUP)]
    tokens = jnp.stack(by_xor(arrived, rank))
    mask = GROUP
    while mask < lax.axis_size("ep"):
        bit = (rank & mask) > 0
        other = swapped(tokens, mask, True)
        tokens = jnp.concatenate(
            [jnp.where(bit, other, tokens), jnp.where(bit, tokens, other)], axis=0
        )
        mask *= 2
    return tokens


def return_tokens(expert_out):
    rank = lax.axis_index("ep")
    peers, tokens, quarter = expert_out.shape
    held = expert_out[:, None]
    mask = peers // 2
    while mask >= GROUP:
        bit = (rank & mask) > 0
        kept = jnp.where(bit, held[mask:], held[:mask])
        other = swapped(jnp.where(bit, held[:mask], held[mask:]), mask, True)
        held = jnp.concatenate(
            [jnp.where(bit, other, kept), jnp.where(bit, kept, other)], axis=1
        )
        mask //= 2
    bits = held.shape[1].bit_length() - 1
    order = [int(format(index, "b").zfill(bits)[::-1], 2) if bits else 0 for index in range(2**bits)]
    leaving = by_xor([held[index] for index in range(GROUP)], rank)
    leaving = lax.optimization_barrier(leaving)
    arrived = [leaving[0]] + [swapped(leaving[mask], mask, True) for mask in (3, 1, 2)]
    arrived = [arrived[index] for index in (0, 2, 3, 1)]
    return [
        jnp.stack([block[order[index]] for index in range(len(order))])
        for block in by_xor(arrived, rank)
    ]


def route_tables(expert_ids, experts, capacity):
    tok_rows, route_count = expert_ids.shape
    flat_ids = expert_ids.reshape(-1)
    expert_hot = (flat_ids[:, None] == jnp.arange(experts, dtype=jnp.int32)[None, :]).astype(
        jnp.int32
    )
    ranking = jnp.sum((jnp.cumsum(expert_hot, axis=0) - expert_hot) * expert_hot, axis=1)
    slot_hot = (ranking[:, None] == jnp.arange(capacity, dtype=jnp.int32)[None, :]).astype(
        jnp.float32
    )
    expert_float = expert_hot.astype(jnp.float32).reshape(tok_rows, route_count, experts)
    return (expert_float, slot_hot.reshape(tok_rows, route_count, capacity))


def expert_rows(rows, w_gate, w_up, w_down):
    hidden_units = w_gate.shape[1]
    weights_in = lax.optimization_barrier(jnp.concatenate([w_gate, w_up], axis=1))
    parts = jnp.dot(rows, weights_in, preferred_element_type=jnp.float32)
    sent = parts.astype(jnp.bfloat16)
    others = [swapped(sent, mask, False) for mask in range(GROUP - 1, 0, -1)]
    for other in others:
        parts = parts + other.astype(jnp.float32)
    inner_rows = (jax.nn.silu(parts[:, :hidden_units]) * parts[:, hidden_units:]).astype(
        jnp.bfloat16
    )
    partial_out = jnp.dot(inner_rows, w_down, preferred_element_type=jnp.float32)
    return core_sum(partial_out).astype(jnp.bfloat16)


def local(hidden, expert_ids, gate_scores, w_gate, w_up, w_down):
    tok_rows, width_all = hidden.shape
    route_count = expert_ids.shape[1]
    peer_count = lax.axis_size("ep")
    experts = peer_count // GROUP
    quarter = width_all // GROUP
    routing = (gate_scores / jnp.sum(gate_scores, axis=1, keepdims=True) * route_scale).astype(
        jnp.bfloat16
    )
    routing = routing.astype(jnp.float32)
    if route_count == experts:
        named = expert_ids[:, :, None] == jnp.arange(experts, dtype=jnp.int32)
        share = jnp.sum(jnp.where(named, routing[:, :, None], 0.0), axis=1)
        rows = spread_tokens(hidden).reshape(peer_count * tok_rows, quarter)
        expert_out = expert_rows(rows, w_gate[0], w_up[0], w_down[0])
        returned = return_tokens(expert_out.reshape(peer_count, tok_rows, quarter))
        combined = jnp.concatenate(
            [
                sum(
                    block[index].astype(jnp.float32) * share[:, index : index + 1]
                    for index in range(experts)
                )
                for block in returned
            ],
            axis=1,
        )
        return combined.astype(jnp.bfloat16)
    capacity = min(tok_rows, 2 * tok_rows * route_count // experts)
    expert_hot, slot_hot = route_tables(expert_ids, experts, capacity)
    placing = jnp.einsum("tke,tkc->ect", expert_hot, slot_hot).astype(jnp.bfloat16)
    outgoing = jnp.einsum(
        "ect,tgd->egcd",
        placing,
        hidden.reshape(tok_rows, GROUP, quarter),
        preferred_element_type=jnp.float32,
    ).astype(jnp.bfloat16)
    outgoing = outgoing.reshape(peer_count, capacity, quarter)
    arrived = lax.all_to_all(outgoing, "ep", split_axis=0, concat_axis=0, tiled=True)
    rows = arrived.reshape(peer_count * capacity, quarter)
    expert_out = expert_rows(rows, w_gate[0], w_up[0], w_down[0])
    returned = lax.all_to_all(
        expert_out.reshape(peer_count, capacity, quarter),
        "ep",
        split_axis=0,
        concat_axis=0,
        tiled=True,
    ).reshape(experts, GROUP, capacity, quarter)
    combining = jnp.einsum("tk,tke,tkc->tec", routing, expert_hot, slot_hot).astype(jnp.bfloat16)
    combined = jnp.einsum(
        "tec,egcd->tgd", combining, returned, preferred_element_type=jnp.float32
    )
    return combined.reshape(tok_rows, width_all).astype(jnp.bfloat16)


def solution(mesh):
    return jax.shard_map(
        local,
        mesh=mesh,
        in_specs=(
            P(("groups", "ep"), None),
            P(("groups", "ep"), None),
            P(("groups", "ep"), None),
            P("ep", None, "tp"),
            P("ep", None, "tp"),
            P("ep", "tp", None),
        ),
        out_specs=P(("groups", "ep"), None),
        check_vma=False,
    )
```

```python
import jax
import jax.numpy as jnp
from jax import lax
from jax.sharding import PartitionSpec as P

GROUP = 4


route_scale = 2.5


def swapped(value, masks, crossed):
    ranks = lax.axis_size("ep")
    cores = lax.axis_size("tp")
    pairs = []
    for source in range(ranks):
        for core in range(cores):
            target_core = (core + 1) % cores if crossed else core
            pairs.append((source * cores + core, (source ^ masks[core]) * cores + target_core))
    return lax.ppermute(value, ("ep", "tp"), pairs)


def same_mask(mask):
    return [mask] * lax.axis_size("tp")


def other_core(value):
    return lax.ppermute(value, "tp", [(0, 1), (1, 0)])


def by_xor(blocks, rank):
    mask = 1
    while mask < len(blocks):
        bit = (rank & mask) > 0
        blocks = [
            jnp.where(bit, blocks[index ^ mask], blocks[index]) for index in range(len(blocks))
        ]
        mask *= 2
    return blocks


def quarters_of(rows):
    quarter = rows.shape[1] // GROUP
    return [rows[:, index * quarter : (index + 1) * quarter] for index in range(GROUP)]


def gathered(outgoing, near, arrive):
    apart = arrive(swapped(outgoing, [2, 3], False))
    close = arrive(swapped(near, same_mask(1), True))
    swap = other_core(apart)
    swap, apart, close = lax.optimization_barrier((swap, apart, close))
    upper = lax.axis_index("tp") == 1
    return [None, close, jnp.where(upper, swap, apart), jnp.where(upper, apart, swap)]


def spread_tokens(hidden):
    rank = lax.axis_index("ep")

    def own_quarter(rows):
        return by_xor(quarters_of(rows), rank)[0]

    blocks = gathered(hidden, hidden, own_quarter)
    blocks[0] = lax.optimization_barrier(own_quarter(hidden))
    tokens = jnp.stack(by_xor(blocks, rank))
    mask = GROUP
    while mask < lax.axis_size("ep"):
        bit = (rank & mask) > 0
        other = swapped(tokens, same_mask(mask), True)
        tokens = jnp.concatenate(
            [jnp.where(bit, other, tokens), jnp.where(bit, tokens, other)], axis=0
        )
        mask *= 2
    return tokens


def return_tokens(expert_out):
    rank = lax.axis_index("ep")
    held = expert_out[:, None]
    mask = GROUP
    while mask < lax.axis_size("ep"):
        bit = (rank & mask) > 0
        pairs = held.reshape((-1, 2, GROUP) + held.shape[1:])
        kept = jnp.where(bit, pairs[:, 1], pairs[:, 0]).reshape((-1,) + held.shape[1:])
        sent = jnp.where(bit, pairs[:, 0], pairs[:, 1]).reshape((-1,) + held.shape[1:])
        other = swapped(sent, same_mask(mask), True)
        held = jnp.concatenate(
            [jnp.where(bit, other, kept), jnp.where(bit, kept, other)], axis=1
        )
        mask *= 2
    leaving = by_xor([held[index] for index in range(GROUP)], rank)
    upper = lax.axis_index("tp") == 1
    own, close, apart = lax.optimization_barrier(
        (leaving[0], leaving[1], jnp.where(upper, leaving[3], leaving[2]))
    )
    blocks = gathered(apart, close, lambda block: block)
    blocks[0] = own
    return by_xor(blocks, rank)


def route_tables(expert_ids, experts, capacity):
    tok_rows, route_count = expert_ids.shape
    flat_ids = expert_ids.reshape(-1)
    expert_hot = (flat_ids[:, None] == jnp.arange(experts, dtype=jnp.int32)[None, :]).astype(
        jnp.int32
    )
    ranking = jnp.sum((jnp.cumsum(expert_hot, axis=0) - expert_hot) * expert_hot, axis=1)
    slot_hot = (ranking[:, None] == jnp.arange(capacity, dtype=jnp.int32)[None, :]).astype(
        jnp.float32
    )
    expert_float = expert_hot.astype(jnp.float32).reshape(tok_rows, route_count, experts)
    return (expert_float, slot_hot.reshape(tok_rows, route_count, capacity))


def expert_rows(rows, w_gate, w_up, w_down):
    hidden_units = w_gate.shape[1]
    weights_in = lax.optimization_barrier(jnp.concatenate([w_gate, w_up], axis=1))
    parts = jnp.dot(rows, weights_in, preferred_element_type=jnp.float32)
    sent = parts.astype(jnp.bfloat16)
    others = [swapped(sent, same_mask(mask), False) for mask in range(GROUP - 1, 0, -1)]
    for other in others:
        parts = parts + other.astype(jnp.float32)
    inner_rows = (jax.nn.silu(parts[:, :hidden_units]) * parts[:, hidden_units:]).astype(
        jnp.bfloat16
    )
    partial_out = jnp.dot(inner_rows, w_down, preferred_element_type=jnp.float32)
    return (partial_out + other_core(partial_out)).astype(jnp.bfloat16)


def local(hidden, expert_ids, gate_scores, w_gate, w_up, w_down):
    tok_rows, width_all = hidden.shape
    route_count = expert_ids.shape[1]
    peer_count = lax.axis_size("ep")
    experts = peer_count // GROUP
    quarter = width_all // GROUP
    routing = (gate_scores / jnp.sum(gate_scores, axis=1, keepdims=True) * route_scale).astype(
        jnp.bfloat16
    )
    routing = routing.astype(jnp.float32)
    if route_count == experts:
        named = expert_ids[:, :, None] == jnp.arange(experts, dtype=jnp.int32)
        share = jnp.sum(jnp.where(named, routing[:, :, None], 0.0), axis=1)
        rows = spread_tokens(hidden).reshape(peer_count * tok_rows, quarter)
        expert_out = expert_rows(rows, w_gate[0], w_up[0], w_down[0])
        returned = return_tokens(expert_out.reshape(peer_count, tok_rows, quarter))
        combined = jnp.concatenate(
            [
                sum(
                    block[index].astype(jnp.float32) * share[:, index : index + 1]
                    for index in range(experts)
                )
                for block in returned
            ],
            axis=1,
        )
        return combined.astype(jnp.bfloat16)
    capacity = min(tok_rows, 2 * tok_rows * route_count // experts)
    expert_hot, slot_hot = route_tables(expert_ids, experts, capacity)
    placing = jnp.einsum("tke,tkc->ect", expert_hot, slot_hot).astype(jnp.bfloat16)
    outgoing = jnp.einsum(
        "ect,tgd->egcd",
        placing,
        hidden.reshape(tok_rows, GROUP, quarter),
        preferred_element_type=jnp.float32,
    ).astype(jnp.bfloat16)
    outgoing = outgoing.reshape(peer_count, capacity, quarter)
    arrived = lax.all_to_all(outgoing, "ep", split_axis=0, concat_axis=0, tiled=True)
    rows = arrived.reshape(peer_count * capacity, quarter)
    expert_out = expert_rows(rows, w_gate[0], w_up[0], w_down[0])
    returned = lax.all_to_all(
        expert_out.reshape(peer_count, capacity, quarter),
        "ep",
        split_axis=0,
        concat_axis=0,
        tiled=True,
    ).reshape(experts, GROUP, capacity, quarter)
    combining = jnp.einsum("tk,tke,tkc->tec", routing, expert_hot, slot_hot).astype(jnp.bfloat16)
    combined = jnp.einsum(
        "tec,egcd->tgd", combining, returned, preferred_element_type=jnp.float32
    )
    return combined.reshape(tok_rows, width_all).astype(jnp.bfloat16)


def solution(mesh):
    return jax.shard_map(
        local,
        mesh=mesh,
        in_specs=(
            P(("groups", "ep"), None),
            P(("groups", "ep"), None),
            P(("groups", "ep"), None),
            P("ep", None, "tp"),
            P("ep", None, "tp"),
            P("ep", "tp", None),
        ),
        out_specs=P(("groups", "ep"), None),
        check_vma=False,
    )
```

```python
import jax
import jax.numpy as jnp
from jax import lax
from jax.sharding import PartitionSpec as P

GROUP = 4


route_scale = 2.5


def swapped(value, masks, crossed):
    ranks = lax.axis_size("ep")
    cores = lax.axis_size("tp")
    pairs = []
    for source in range(ranks):
        for core in range(cores):
            target_core = (core + 1) % cores if crossed else core
            pairs.append((source * cores + core, (source ^ masks[core]) * cores + target_core))
    return lax.ppermute(value, ("ep", "tp"), pairs)


def same_mask(mask):
    return [mask] * lax.axis_size("tp")


def other_core(value):
    return lax.ppermute(value, "tp", [(0, 1), (1, 0)])


def by_xor(blocks, rank):
    mask = 1
    while mask < len(blocks):
        bit = (rank & mask) > 0
        blocks = [
            jnp.where(bit, blocks[index ^ mask], blocks[index]) for index in range(len(blocks))
        ]
        mask *= 2
    return blocks


def quarters_of(rows):
    quarter = rows.shape[1] // GROUP
    return [rows[:, index * quarter : (index + 1) * quarter] for index in range(GROUP)]


def gathered(split, masks, crossed, shared, shared_crossed, arrive):
    third = masks[0] ^ masks[1]
    got = arrive(swapped(split, masks, crossed))
    both = arrive(swapped(shared, same_mask(third), shared_crossed))
    swap = other_core(got)
    swap, got, both = lax.optimization_barrier((swap, got, both))
    upper = lax.axis_index("tp") == 1
    lower_mask, upper_mask = reversed(masks) if crossed else masks
    return {
        third: both,
        lower_mask: jnp.where(upper, swap, got),
        upper_mask: jnp.where(upper, got, swap),
    }


def spread_tokens(hidden):
    rank = lax.axis_index("ep")

    def own_quarter(rows):
        return by_xor(quarters_of(rows), rank)[0]

    blocks = gathered(hidden, [3, 2], True, hidden, True, own_quarter)
    blocks[0] = lax.optimization_barrier(own_quarter(hidden))
    tokens = jnp.stack(by_xor([blocks[index] for index in range(GROUP)], rank))
    mask = GROUP
    while mask < lax.axis_size("ep"):
        bit = (rank & mask) > 0
        other = swapped(tokens, same_mask(mask), True)
        tokens = jnp.concatenate(
            [jnp.where(bit, other, tokens), jnp.where(bit, tokens, other)], axis=0
        )
        mask *= 2
    return tokens


def return_tokens(expert_out):
    rank = lax.axis_index("ep")
    held = expert_out[:, None]
    mask = GROUP
    while mask < lax.axis_size("ep"):
        bit = (rank & mask) > 0
        pairs = held.reshape((-1, 2, GROUP) + held.shape[1:])
        kept = jnp.where(bit, pairs[:, 1], pairs[:, 0]).reshape((-1,) + held.shape[1:])
        sent = jnp.where(bit, pairs[:, 0], pairs[:, 1]).reshape((-1,) + held.shape[1:])
        other = swapped(sent, same_mask(mask), True)
        held = jnp.concatenate(
            [jnp.where(bit, other, kept), jnp.where(bit, kept, other)], axis=1
        )
        mask *= 2
    leaving = by_xor([held[index] for index in range(GROUP)], rank)
    upper = lax.axis_index("tp") == 1
    masks = [1, 3]
    own, shared, split = lax.optimization_barrier(
        (leaving[0], leaving[2], jnp.where(upper, leaving[masks[1]], leaving[masks[0]]))
    )
    blocks = gathered(split, masks, False, shared, False, lambda block: block)
    blocks[0] = own
    return by_xor([blocks[index] for index in range(GROUP)], rank)


def route_tables(expert_ids, experts, capacity):
    tok_rows, route_count = expert_ids.shape
    flat_ids = expert_ids.reshape(-1)
    expert_hot = (flat_ids[:, None] == jnp.arange(experts, dtype=jnp.int32)[None, :]).astype(
        jnp.int32
    )
    ranking = jnp.sum((jnp.cumsum(expert_hot, axis=0) - expert_hot) * expert_hot, axis=1)
    slot_hot = (ranking[:, None] == jnp.arange(capacity, dtype=jnp.int32)[None, :]).astype(
        jnp.float32
    )
    expert_float = expert_hot.astype(jnp.float32).reshape(tok_rows, route_count, experts)
    return (expert_float, slot_hot.reshape(tok_rows, route_count, capacity))


def expert_rows(rows, w_gate, w_up, w_down):
    hidden_units = w_gate.shape[1]
    weights_in = lax.optimization_barrier(jnp.concatenate([w_gate, w_up], axis=1))
    parts = jnp.dot(rows, weights_in, preferred_element_type=jnp.float32)
    sent = parts.astype(jnp.bfloat16)
    others = [swapped(sent, same_mask(mask), False) for mask in range(GROUP - 1, 0, -1)]
    for other in others:
        parts = parts + other.astype(jnp.float32)
    inner_rows = (jax.nn.silu(parts[:, :hidden_units]) * parts[:, hidden_units:]).astype(
        jnp.bfloat16
    )
    partial_out = jnp.dot(inner_rows, w_down, preferred_element_type=jnp.float32)
    return (partial_out + other_core(partial_out)).astype(jnp.bfloat16)


def local(hidden, expert_ids, gate_scores, w_gate, w_up, w_down):
    tok_rows, width_all = hidden.shape
    route_count = expert_ids.shape[1]
    peer_count = lax.axis_size("ep")
    experts = peer_count // GROUP
    quarter = width_all // GROUP
    routing = (gate_scores / jnp.sum(gate_scores, axis=1, keepdims=True) * route_scale).astype(
        jnp.bfloat16
    )
    routing = routing.astype(jnp.float32)
    if route_count == experts:
        named = expert_ids[:, :, None] == jnp.arange(experts, dtype=jnp.int32)
        share = jnp.sum(jnp.where(named, routing[:, :, None], 0.0), axis=1)
        rows = spread_tokens(hidden).reshape(peer_count * tok_rows, quarter)
        expert_out = expert_rows(rows, w_gate[0], w_up[0], w_down[0])
        returned = return_tokens(expert_out.reshape(peer_count, tok_rows, quarter))
        combined = jnp.concatenate(
            [
                sum(
                    block[index].astype(jnp.float32) * share[:, index : index + 1]
                    for index in range(experts)
                )
                for block in returned
            ],
            axis=1,
        )
        return combined.astype(jnp.bfloat16)
    capacity = min(tok_rows, 2 * tok_rows * route_count // experts)
    expert_hot, slot_hot = route_tables(expert_ids, experts, capacity)
    placing = jnp.einsum("tke,tkc->ect", expert_hot, slot_hot).astype(jnp.bfloat16)
    outgoing = jnp.einsum(
        "ect,tgd->egcd",
        placing,
        hidden.reshape(tok_rows, GROUP, quarter),
        preferred_element_type=jnp.float32,
    ).astype(jnp.bfloat16)
    outgoing = outgoing.reshape(peer_count, capacity, quarter)
    arrived = lax.all_to_all(outgoing, "ep", split_axis=0, concat_axis=0, tiled=True)
    rows = arrived.reshape(peer_count * capacity, quarter)
    expert_out = expert_rows(rows, w_gate[0], w_up[0], w_down[0])
    returned = lax.all_to_all(
        expert_out.reshape(peer_count, capacity, quarter),
        "ep",
        split_axis=0,
        concat_axis=0,
        tiled=True,
    ).reshape(experts, GROUP, capacity, quarter)
    combining = jnp.einsum("tk,tke,tkc->tec", routing, expert_hot, slot_hot).astype(jnp.bfloat16)
    combined = jnp.einsum(
        "tec,egcd->tgd", combining, returned, preferred_element_type=jnp.float32
    )
    return combined.reshape(tok_rows, width_all).astype(jnp.bfloat16)


def solution(mesh):
    return jax.shard_map(
        local,
        mesh=mesh,
        in_specs=(
            P(("groups", "ep"), None),
            P(("groups", "ep"), None),
            P(("groups", "ep"), None),
            P("ep", None, "tp"),
            P("ep", None, "tp"),
            P("ep", "tp", None),
        ),
        out_specs=P(("groups", "ep"), None),
        check_vma=False,
    )
```

```python
import jax
import jax.numpy as jnp
from jax import lax
from jax.sharding import PartitionSpec as P

GROUP = 4


route_scale = 2.5


def swapped(value, masks, crossed):
    ranks = lax.axis_size("ep")
    cores = lax.axis_size("tp")
    pairs = []
    for source in range(ranks):
        for core in range(cores):
            target_core = (core + 1) % cores if crossed else core
            pairs.append((source * cores + core, (source ^ masks[core]) * cores + target_core))
    return lax.ppermute(value, ("ep", "tp"), pairs)


def same_mask(mask):
    return [mask] * lax.axis_size("tp")


def other_core(value):
    return lax.ppermute(value, "tp", [(0, 1), (1, 0)])


def by_xor(blocks, rank):
    mask = 1
    while mask < len(blocks):
        bit = (rank & mask) > 0
        blocks = [
            jnp.where(bit, blocks[index ^ mask], blocks[index]) for index in range(len(blocks))
        ]
        mask *= 2
    return blocks


def quarters_of(rows):
    quarter = rows.shape[1] // GROUP
    return [rows[:, index * quarter : (index + 1) * quarter] for index in range(GROUP)]


def gathered(split, masks, crossed, shared, shared_crossed, arrive):
    third = masks[0] ^ masks[1]
    got = arrive(swapped(split, masks, crossed))
    both = arrive(swapped(shared, same_mask(third), shared_crossed))
    swap = other_core(got)
    swap, got, both = lax.optimization_barrier((swap, got, both))
    upper = lax.axis_index("tp") == 1
    lower_mask, upper_mask = reversed(masks) if crossed else masks
    return {
        third: both,
        lower_mask: jnp.where(upper, swap, got),
        upper_mask: jnp.where(upper, got, swap),
    }


def spread_tokens(hidden):
    rank = lax.axis_index("ep")

    def own_quarter(rows):
        return by_xor(quarters_of(rows), rank)[0]

    blocks = gathered(hidden, [3, 2], True, hidden, True, own_quarter)
    blocks[0] = lax.optimization_barrier(own_quarter(hidden))
    tokens = jnp.stack(by_xor([blocks[index] for index in range(GROUP)], rank))
    mask = GROUP
    while mask < lax.axis_size("ep"):
        tokens = jnp.concatenate([tokens, swapped(tokens, same_mask(mask), True)], axis=0)
        mask *= 2
    return tokens


def return_tokens(expert_out):
    rank = lax.axis_index("ep")
    held = expert_out[:, None]
    mask = GROUP
    while mask < lax.axis_size("ep"):
        pairs = held.reshape((-1, 2, GROUP) + held.shape[1:])
        kept = pairs[:, 0].reshape((-1,) + held.shape[1:])
        sent = pairs[:, 1].reshape((-1,) + held.shape[1:])
        held = jnp.concatenate([kept, swapped(sent, same_mask(mask), True)], axis=1)
        mask *= 2
    leaving = by_xor([held[index] for index in range(GROUP)], rank)
    upper = lax.axis_index("tp") == 1
    masks = [1, 3]
    own, shared, split = lax.optimization_barrier(
        (leaving[0], leaving[2], jnp.where(upper, leaving[masks[1]], leaving[masks[0]]))
    )
    blocks = gathered(split, masks, False, shared, False, lambda block: block)
    blocks[0] = own
    return by_xor([blocks[index] for index in range(GROUP)], rank)


def route_tables(expert_ids, experts, capacity):
    tok_rows, route_count = expert_ids.shape
    flat_ids = expert_ids.reshape(-1)
    expert_hot = (flat_ids[:, None] == jnp.arange(experts, dtype=jnp.int32)[None, :]).astype(
        jnp.int32
    )
    ranking = jnp.sum((jnp.cumsum(expert_hot, axis=0) - expert_hot) * expert_hot, axis=1)
    slot_hot = (ranking[:, None] == jnp.arange(capacity, dtype=jnp.int32)[None, :]).astype(
        jnp.float32
    )
    expert_float = expert_hot.astype(jnp.float32).reshape(tok_rows, route_count, experts)
    return (expert_float, slot_hot.reshape(tok_rows, route_count, capacity))


def expert_rows(rows, w_gate, w_up, w_down):
    hidden_units = w_gate.shape[1]
    weights_in = lax.optimization_barrier(jnp.concatenate([w_gate, w_up], axis=1))
    parts = jnp.dot(rows, weights_in, preferred_element_type=jnp.float32)
    sent = parts.astype(jnp.bfloat16)
    others = [swapped(sent, same_mask(mask), False) for mask in range(GROUP - 1, 0, -1)]
    for other in others:
        parts = parts + other.astype(jnp.float32)
    inner_rows = (jax.nn.silu(parts[:, :hidden_units]) * parts[:, hidden_units:]).astype(
        jnp.bfloat16
    )
    partial_out = jnp.dot(inner_rows, w_down, preferred_element_type=jnp.float32)
    return (partial_out + other_core(partial_out)).astype(jnp.bfloat16)


def local(hidden, expert_ids, gate_scores, w_gate, w_up, w_down):
    tok_rows, width_all = hidden.shape
    route_count = expert_ids.shape[1]
    peer_count = lax.axis_size("ep")
    experts = peer_count // GROUP
    quarter = width_all // GROUP
    routing = (gate_scores / jnp.sum(gate_scores, axis=1, keepdims=True) * route_scale).astype(
        jnp.bfloat16
    )
    routing = routing.astype(jnp.float32)
    if route_count == experts:
        named = expert_ids[:, :, None] == jnp.arange(experts, dtype=jnp.int32)
        share = jnp.sum(jnp.where(named, routing[:, :, None], 0.0), axis=1)
        rows = spread_tokens(hidden).reshape(peer_count * tok_rows, quarter)
        expert_out = expert_rows(rows, w_gate[0], w_up[0], w_down[0])
        returned = return_tokens(expert_out.reshape(peer_count, tok_rows, quarter))
        shares = [share[:, index : index + 1] for index in range(experts)]
        shares = by_xor(shares, lax.axis_index("ep") // GROUP)
        combined = sum(
            jnp.concatenate([block[index] for block in returned], axis=1).astype(jnp.float32)
            * shares[index]
            for index in range(experts)
        )
        return combined.astype(jnp.bfloat16)
    capacity = min(tok_rows, 2 * tok_rows * route_count // experts)
    expert_hot, slot_hot = route_tables(expert_ids, experts, capacity)
    placing = jnp.einsum("tke,tkc->ect", expert_hot, slot_hot).astype(jnp.bfloat16)
    outgoing = jnp.einsum(
        "ect,tgd->egcd",
        placing,
        hidden.reshape(tok_rows, GROUP, quarter),
        preferred_element_type=jnp.float32,
    ).astype(jnp.bfloat16)
    outgoing = outgoing.reshape(peer_count, capacity, quarter)
    arrived = lax.all_to_all(outgoing, "ep", split_axis=0, concat_axis=0, tiled=True)
    rows = arrived.reshape(peer_count * capacity, quarter)
    expert_out = expert_rows(rows, w_gate[0], w_up[0], w_down[0])
    returned = lax.all_to_all(
        expert_out.reshape(peer_count, capacity, quarter),
        "ep",
        split_axis=0,
        concat_axis=0,
        tiled=True,
    ).reshape(experts, GROUP, capacity, quarter)
    combining = jnp.einsum("tk,tke,tkc->tec", routing, expert_hot, slot_hot).astype(jnp.bfloat16)
    combined = jnp.einsum(
        "tec,egcd->tgd", combining, returned, preferred_element_type=jnp.float32
    )
    return combined.reshape(tok_rows, width_all).astype(jnp.bfloat16)


def solution(mesh):
    return jax.shard_map(
        local,
        mesh=mesh,
        in_specs=(
            P(("groups", "ep"), None),
            P(("groups", "ep"), None),
            P(("groups", "ep"), None),
            P("ep", None, "tp"),
            P("ep", None, "tp"),
            P("ep", "tp", None),
        ),
        out_specs=P(("groups", "ep"), None),
        check_vma=False,
    )
```

```python
import jax
import jax.numpy as jnp
from jax import lax
from jax.sharding import PartitionSpec as P

GROUP = 4


route_scale = 2.5


def swapped(value, masks, crossed):
    ranks = lax.axis_size("ep")
    cores = lax.axis_size("tp")
    pairs = []
    for source in range(ranks):
        for core in range(cores):
            target_core = (core + 1) % cores if crossed else core
            pairs.append((source * cores + core, (source ^ masks[core]) * cores + target_core))
    return lax.ppermute(value, ("ep", "tp"), pairs)


def same_mask(mask):
    return [mask] * lax.axis_size("tp")


def other_core(value):
    return lax.ppermute(value, "tp", [(0, 1), (1, 0)])


def by_xor(blocks, rank):
    mask = 1
    while mask < len(blocks):
        bit = (rank & mask) > 0
        blocks = [
            jnp.where(bit, blocks[index ^ mask], blocks[index]) for index in range(len(blocks))
        ]
        mask *= 2
    return blocks


def quarters_of(rows):
    quarter = rows.shape[1] // GROUP
    return [rows[:, index * quarter : (index + 1) * quarter] for index in range(GROUP)]


def gathered(split, masks, crossed, shared, shared_crossed, arrive):
    third = masks[0] ^ masks[1]
    got = arrive(swapped(split, masks, crossed))
    both = arrive(swapped(shared, same_mask(third), shared_crossed))
    swap = other_core(got)
    swap, got, both = lax.optimization_barrier((swap, got, both))
    upper = lax.axis_index("tp") == 1
    lower_mask, upper_mask = reversed(masks) if crossed else masks
    return {
        third: both,
        lower_mask: jnp.where(upper, swap, got),
        upper_mask: jnp.where(upper, got, swap),
    }


def spread_tokens(hidden):
    rank = lax.axis_index("ep")

    def own_quarter(rows):
        return by_xor(quarters_of(rows), rank)[0]

    blocks = gathered(hidden, [3, 2], True, hidden, True, own_quarter)
    blocks[0] = lax.optimization_barrier(own_quarter(hidden))
    tokens = jnp.stack(by_xor([blocks[index] for index in range(GROUP)], rank))
    mask = GROUP
    while mask < lax.axis_size("ep"):
        tokens = jnp.concatenate([tokens, swapped(tokens, same_mask(mask), True)], axis=0)
        mask *= 2
    return tokens


def return_tokens(near, far):
    rank = lax.axis_index("ep")
    held = near[:, None]
    mask = GROUP
    if mask * 2 == lax.axis_size("ep"):
        other = swapped(far[:, None], same_mask(mask), True)
        other, held = lax.optimization_barrier((other, held))
        held = jnp.concatenate([held, other], axis=1)
        mask *= 2
    else:
        held = jnp.concatenate([near, far])[:, None]
    while mask < lax.axis_size("ep"):
        pairs = held.reshape((-1, 2, GROUP) + held.shape[1:])
        kept = pairs[:, 0].reshape((-1,) + held.shape[1:])
        sent = pairs[:, 1].reshape((-1,) + held.shape[1:])
        held = jnp.concatenate([kept, swapped(sent, same_mask(mask), True)], axis=1)
        mask *= 2
    leaving = by_xor([held[index] for index in range(GROUP)], rank)
    upper = lax.axis_index("tp") == 1
    masks = [1, 3]
    own, shared, split = lax.optimization_barrier(
        (leaving[0], leaving[2], jnp.where(upper, leaving[masks[1]], leaving[masks[0]]))
    )
    blocks = gathered(split, masks, False, shared, False, lambda block: block)
    blocks[0] = own
    return by_xor([blocks[index] for index in range(GROUP)], rank)


def route_tables(expert_ids, experts, capacity):
    tok_rows, route_count = expert_ids.shape
    flat_ids = expert_ids.reshape(-1)
    expert_hot = (flat_ids[:, None] == jnp.arange(experts, dtype=jnp.int32)[None, :]).astype(
        jnp.int32
    )
    ranking = jnp.sum((jnp.cumsum(expert_hot, axis=0) - expert_hot) * expert_hot, axis=1)
    slot_hot = (ranking[:, None] == jnp.arange(capacity, dtype=jnp.int32)[None, :]).astype(
        jnp.float32
    )
    expert_float = expert_hot.astype(jnp.float32).reshape(tok_rows, route_count, experts)
    return (expert_float, slot_hot.reshape(tok_rows, route_count, capacity))


def expert_rows(rows, w_gate, w_up, w_down, groups=0):
    hidden_units = w_gate.shape[1]
    weights_in = lax.optimization_barrier(jnp.concatenate([w_gate, w_up], axis=1))
    parts = jnp.dot(rows, weights_in, preferred_element_type=jnp.float32)
    sent = parts.astype(jnp.bfloat16)
    others = [swapped(sent, same_mask(mask), False) for mask in range(GROUP - 1, 0, -1)]
    for other in others:
        parts = parts + other.astype(jnp.float32)
    inner_rows = (jax.nn.silu(parts[:, :hidden_units]) * parts[:, hidden_units:]).astype(
        jnp.bfloat16
    )
    partial_out = jnp.dot(inner_rows, w_down, preferred_element_type=jnp.float32)
    if not groups:
        return (partial_out + other_core(partial_out)).astype(jnp.bfloat16)
    own_rows = partial_out.shape[0] // groups
    near, far = partial_out[:own_rows], partial_out[own_rows:]
    near, far = lax.optimization_barrier((near, far))
    far_sum = (far + other_core(far)).astype(jnp.bfloat16)
    near_sum = (near + other_core(near)).astype(jnp.bfloat16)
    return near_sum, far_sum


def local(hidden, expert_ids, gate_scores, w_gate, w_up, w_down):
    tok_rows, width_all = hidden.shape
    route_count = expert_ids.shape[1]
    peer_count = lax.axis_size("ep")
    experts = peer_count // GROUP
    quarter = width_all // GROUP
    routing = (gate_scores / jnp.sum(gate_scores, axis=1, keepdims=True) * route_scale).astype(
        jnp.bfloat16
    )
    routing = routing.astype(jnp.float32)
    if route_count == experts:
        named = expert_ids[:, :, None] == jnp.arange(experts, dtype=jnp.int32)
        share = jnp.sum(jnp.where(named, routing[:, :, None], 0.0), axis=1)
        rows = spread_tokens(hidden).reshape(peer_count * tok_rows, quarter)
        near, far = expert_rows(rows, w_gate[0], w_up[0], w_down[0], experts)
        returned = return_tokens(
            near.reshape(-1, tok_rows, quarter), far.reshape(-1, tok_rows, quarter)
        )
        shares = [share[:, index : index + 1] for index in range(experts)]
        shares = by_xor(shares, lax.axis_index("ep") // GROUP)
        combined = sum(
            jnp.concatenate([block[index] for block in returned], axis=1).astype(jnp.float32)
            * shares[index]
            for index in range(experts)
        )
        return combined.astype(jnp.bfloat16)
    capacity = min(tok_rows, 2 * tok_rows * route_count // experts)
    expert_hot, slot_hot = route_tables(expert_ids, experts, capacity)
    placing = jnp.einsum("tke,tkc->ect", expert_hot, slot_hot).astype(jnp.bfloat16)
    outgoing = jnp.einsum(
        "ect,tgd->egcd",
        placing,
        hidden.reshape(tok_rows, GROUP, quarter),
        preferred_element_type=jnp.float32,
    ).astype(jnp.bfloat16)
    outgoing = outgoing.reshape(peer_count, capacity, quarter)
    arrived = lax.all_to_all(outgoing, "ep", split_axis=0, concat_axis=0, tiled=True)
    rows = arrived.reshape(peer_count * capacity, quarter)
    expert_out = expert_rows(rows, w_gate[0], w_up[0], w_down[0])
    returned = lax.all_to_all(
        expert_out.reshape(peer_count, capacity, quarter),
        "ep",
        split_axis=0,
        concat_axis=0,
        tiled=True,
    ).reshape(experts, GROUP, capacity, quarter)
    combining = jnp.einsum("tk,tke,tkc->tec", routing, expert_hot, slot_hot).astype(jnp.bfloat16)
    combined = jnp.einsum(
        "tec,egcd->tgd", combining, returned, preferred_element_type=jnp.float32
    )
    return combined.reshape(tok_rows, width_all).astype(jnp.bfloat16)


def solution(mesh):
    return jax.shard_map(
        local,
        mesh=mesh,
        in_specs=(
            P(("groups", "ep"), None),
            P(("groups", "ep"), None),
            P(("groups", "ep"), None),
            P("ep", None, "tp"),
            P("ep", None, "tp"),
            P("ep", "tp", None),
        ),
        out_specs=P(("groups", "ep"), None),
        check_vma=False,
    )
```

```python
import jax
import jax.numpy as jnp
from jax import lax
from jax.sharding import PartitionSpec as P

GROUP = 4


route_scale = 2.5


def swapped(value, masks, crossed):
    ranks = lax.axis_size("ep")
    cores = lax.axis_size("tp")
    pairs = []
    for source in range(ranks):
        for core in range(cores):
            target_core = (core + 1) % cores if crossed else core
            pairs.append((source * cores + core, (source ^ masks[core]) * cores + target_core))
    return lax.ppermute(value, ("ep", "tp"), pairs)


def same_mask(mask):
    return [mask] * lax.axis_size("tp")


def other_core(value):
    return lax.ppermute(value, "tp", [(0, 1), (1, 0)])


def by_xor(blocks, rank):
    mask = 1
    while mask < len(blocks):
        bit = (rank & mask) > 0
        blocks = [
            jnp.where(bit, blocks[index ^ mask], blocks[index]) for index in range(len(blocks))
        ]
        mask *= 2
    return blocks


def quarters_of(rows):
    quarter = rows.shape[1] // GROUP
    return [rows[:, index * quarter : (index + 1) * quarter] for index in range(GROUP)]


def gathered(split, masks, crossed, shared, shared_crossed, arrive):
    third = masks[0] ^ masks[1]
    got = arrive(swapped(split, masks, crossed))
    both = arrive(swapped(shared, same_mask(third), shared_crossed))
    swap = other_core(got)
    swap, got, both = lax.optimization_barrier((swap, got, both))
    upper = lax.axis_index("tp") == 1
    lower_mask, upper_mask = reversed(masks) if crossed else masks
    return {
        third: both,
        lower_mask: jnp.where(upper, swap, got),
        upper_mask: jnp.where(upper, got, swap),
    }


def spread_tokens(hidden):
    rank = lax.axis_index("ep")

    def own_quarter(rows):
        return by_xor(quarters_of(rows), rank)[0]

    blocks = gathered(hidden, [3, 1], True, hidden, True, own_quarter)
    blocks[0] = lax.optimization_barrier(own_quarter(hidden))
    tokens = jnp.stack(by_xor([blocks[index] for index in range(GROUP)], rank))
    mask = GROUP
    while mask < lax.axis_size("ep"):
        tokens = jnp.concatenate([tokens, swapped(tokens, same_mask(mask), True)], axis=0)
        mask *= 2
    return tokens


def return_tokens(near, far):
    rank = lax.axis_index("ep")
    held = near[:, None]
    mask = GROUP
    if mask * 2 == lax.axis_size("ep"):
        other = swapped(far[:, None], same_mask(mask), True)
        other, held = lax.optimization_barrier((other, held))
        held = jnp.concatenate([held, other], axis=1)
        mask *= 2
    else:
        held = jnp.concatenate([near, far])[:, None]
    while mask < lax.axis_size("ep"):
        pairs = held.reshape((-1, 2, GROUP) + held.shape[1:])
        kept = pairs[:, 0].reshape((-1,) + held.shape[1:])
        sent = pairs[:, 1].reshape((-1,) + held.shape[1:])
        held = jnp.concatenate([kept, swapped(sent, same_mask(mask), True)], axis=1)
        mask *= 2
    leaving = by_xor([held[index] for index in range(GROUP)], rank)
    upper = lax.axis_index("tp") == 1
    masks = [1, 3]
    own, shared, split = lax.optimization_barrier(
        (leaving[0], leaving[2], jnp.where(upper, leaving[masks[1]], leaving[masks[0]]))
    )
    blocks = gathered(split, masks, False, shared, False, lambda block: block)
    blocks[0] = own
    return by_xor([blocks[index] for index in range(GROUP)], rank)


def route_tables(expert_ids, experts, capacity):
    tok_rows, route_count = expert_ids.shape
    flat_ids = expert_ids.reshape(-1)
    expert_hot = (flat_ids[:, None] == jnp.arange(experts, dtype=jnp.int32)[None, :]).astype(
        jnp.int32
    )
    ranking = jnp.sum((jnp.cumsum(expert_hot, axis=0) - expert_hot) * expert_hot, axis=1)
    slot_hot = (ranking[:, None] == jnp.arange(capacity, dtype=jnp.int32)[None, :]).astype(
        jnp.float32
    )
    expert_float = expert_hot.astype(jnp.float32).reshape(tok_rows, route_count, experts)
    return (expert_float, slot_hot.reshape(tok_rows, route_count, capacity))


def expert_rows(rows, w_gate, w_up, w_down, groups=0):
    hidden_units = w_gate.shape[1]
    weights_in = lax.optimization_barrier(jnp.concatenate([w_gate, w_up], axis=1))
    parts = jnp.dot(rows, weights_in, preferred_element_type=jnp.float32)
    sent = parts.astype(jnp.bfloat16)
    others = [swapped(sent, same_mask(mask), False) for mask in range(GROUP - 1, 0, -1)]
    for other in others:
        parts = parts + other.astype(jnp.float32)
    inner_rows = (jax.nn.silu(parts[:, :hidden_units]) * parts[:, hidden_units:]).astype(
        jnp.bfloat16
    )
    partial_out = jnp.dot(inner_rows, w_down, preferred_element_type=jnp.float32)
    if not groups:
        return (partial_out + other_core(partial_out)).astype(jnp.bfloat16)
    own_rows = partial_out.shape[0] // groups
    near, far = partial_out[:own_rows], partial_out[own_rows:]
    near, far = lax.optimization_barrier((near, far))
    far_sum = (far + other_core(far)).astype(jnp.bfloat16)
    near_sum = (near + other_core(near)).astype(jnp.bfloat16)
    return near_sum, far_sum


def local(hidden, expert_ids, gate_scores, w_gate, w_up, w_down):
    tok_rows, width_all = hidden.shape
    route_count = expert_ids.shape[1]
    peer_count = lax.axis_size("ep")
    experts = peer_count // GROUP
    quarter = width_all // GROUP
    routing = (gate_scores / jnp.sum(gate_scores, axis=1, keepdims=True) * route_scale).astype(
        jnp.bfloat16
    )
    routing = routing.astype(jnp.float32)
    if route_count == experts:
        named = expert_ids[:, :, None] == jnp.arange(experts, dtype=jnp.int32)
        share = jnp.sum(jnp.where(named, routing[:, :, None], 0.0), axis=1)
        rows = spread_tokens(hidden).reshape(peer_count * tok_rows, quarter)
        near, far = expert_rows(rows, w_gate[0], w_up[0], w_down[0], experts)
        returned = return_tokens(
            near.reshape(-1, tok_rows, quarter), far.reshape(-1, tok_rows, quarter)
        )
        shares = [share[:, index : index + 1] for index in range(experts)]
        shares = by_xor(shares, lax.axis_index("ep") // GROUP)
        combined = sum(
            jnp.concatenate([block[index] for block in returned], axis=1).astype(jnp.float32)
            * shares[index]
            for index in range(experts)
        )
        return combined.astype(jnp.bfloat16)
    capacity = min(tok_rows, 2 * tok_rows * route_count // experts)
    expert_hot, slot_hot = route_tables(expert_ids, experts, capacity)
    placing = jnp.einsum("tke,tkc->ect", expert_hot, slot_hot).astype(jnp.bfloat16)
    outgoing = jnp.einsum(
        "ect,tgd->egcd",
        placing,
        hidden.reshape(tok_rows, GROUP, quarter),
        preferred_element_type=jnp.float32,
    ).astype(jnp.bfloat16)
    outgoing = outgoing.reshape(peer_count, capacity, quarter)
    arrived = lax.all_to_all(outgoing, "ep", split_axis=0, concat_axis=0, tiled=True)
    rows = arrived.reshape(peer_count * capacity, quarter)
    expert_out = expert_rows(rows, w_gate[0], w_up[0], w_down[0])
    returned = lax.all_to_all(
        expert_out.reshape(peer_count, capacity, quarter),
        "ep",
        split_axis=0,
        concat_axis=0,
        tiled=True,
    ).reshape(experts, GROUP, capacity, quarter)
    combining = jnp.einsum("tk,tke,tkc->tec", routing, expert_hot, slot_hot).astype(jnp.bfloat16)
    combined = jnp.einsum(
        "tec,egcd->tgd", combining, returned, preferred_element_type=jnp.float32
    )
    return combined.reshape(tok_rows, width_all).astype(jnp.bfloat16)


def solution(mesh):
    return jax.shard_map(
        local,
        mesh=mesh,
        in_specs=(
            P(("groups", "ep"), None),
            P(("groups", "ep"), None),
            P(("groups", "ep"), None),
            P("ep", None, "tp"),
            P("ep", None, "tp"),
            P("ep", "tp", None),
        ),
        out_specs=P(("groups", "ep"), None),
        check_vma=False,
    )
```

```python
import jax
import jax.numpy as jnp
from jax import lax
from jax.sharding import PartitionSpec as P

GROUP = 4


route_scale = 2.5


def swapped(value, masks, crossed):
    ranks = lax.axis_size("ep")
    cores = lax.axis_size("tp")
    pairs = []
    for source in range(ranks):
        for core in range(cores):
            target_core = (core + 1) % cores if crossed else core
            pairs.append((source * cores + core, (source ^ masks[core]) * cores + target_core))
    return lax.ppermute(value, ("ep", "tp"), pairs)


def same_mask(mask):
    return [mask] * lax.axis_size("tp")


def other_core(value):
    return lax.ppermute(value, "tp", [(0, 1), (1, 0)])


def by_xor(blocks, rank):
    mask = 1
    while mask < len(blocks):
        bit = (rank & mask) > 0
        blocks = [
            jnp.where(bit, blocks[index ^ mask], blocks[index]) for index in range(len(blocks))
        ]
        mask *= 2
    return blocks


def quarters_of(rows):
    quarter = rows.shape[1] // GROUP
    return [rows[:, index * quarter : (index + 1) * quarter] for index in range(GROUP)]


def gathered(split, masks, crossed, shared, shared_crossed, arrive):
    third = masks[0] ^ masks[1]
    got = arrive(swapped(split, masks, crossed))
    both = arrive(swapped(shared, same_mask(third), shared_crossed))
    swap = other_core(got)
    swap, got, both = lax.optimization_barrier((swap, got, both))
    upper = lax.axis_index("tp") == 1
    lower_mask, upper_mask = reversed(masks) if crossed else masks
    return {
        third: both,
        lower_mask: jnp.where(upper, swap, got),
        upper_mask: jnp.where(upper, got, swap),
    }


def spread_tokens(hidden):
    rank = lax.axis_index("ep")

    def own_quarter(rows):
        return by_xor(quarters_of(rows), rank)[0]

    blocks = gathered(hidden, [3, 1], True, hidden, True, own_quarter)
    blocks[0] = lax.optimization_barrier(own_quarter(hidden))
    tokens = jnp.stack(by_xor([blocks[index] for index in range(GROUP)], rank))
    mask = GROUP
    while mask < lax.axis_size("ep"):
        tokens = jnp.concatenate([tokens, swapped(tokens, same_mask(mask), True)], axis=0)
        mask *= 2
    return tokens


def return_tokens(near, far, weighted):
    rank = lax.axis_index("ep")
    held = near[:, None]
    mask = GROUP
    if mask * 2 == lax.axis_size("ep"):
        other = swapped(far[:, None], same_mask(mask), True)
        other, held = lax.optimization_barrier((other, held))
        held = jnp.concatenate([held, other], axis=1)
        mask *= 2
    else:
        held = jnp.concatenate([near, far])[:, None]
    while mask < lax.axis_size("ep"):
        pairs = held.reshape((-1, 2, GROUP) + held.shape[1:])
        kept = pairs[:, 0].reshape((-1,) + held.shape[1:])
        sent = pairs[:, 1].reshape((-1,) + held.shape[1:])
        held = jnp.concatenate([kept, swapped(sent, same_mask(mask), True)], axis=1)
        mask *= 2
    leaving = by_xor([held[index] for index in range(GROUP)], rank)
    upper = lax.axis_index("tp") == 1
    masks = [1, 3]
    own, shared, split = lax.optimization_barrier(
        (leaving[0], leaving[2], jnp.where(upper, leaving[masks[1]], leaving[masks[0]]))
    )
    blocks = gathered(split, masks, False, shared, False, lambda block: block)
    blocks[0] = own
    blocks = {mask: weighted(block) for mask, block in blocks.items()}
    return by_xor([blocks[index] for index in range(GROUP)], rank)


def route_tables(expert_ids, experts, capacity):
    tok_rows, route_count = expert_ids.shape
    flat_ids = expert_ids.reshape(-1)
    expert_hot = (flat_ids[:, None] == jnp.arange(experts, dtype=jnp.int32)[None, :]).astype(
        jnp.int32
    )
    ranking = jnp.sum((jnp.cumsum(expert_hot, axis=0) - expert_hot) * expert_hot, axis=1)
    slot_hot = (ranking[:, None] == jnp.arange(capacity, dtype=jnp.int32)[None, :]).astype(
        jnp.float32
    )
    expert_float = expert_hot.astype(jnp.float32).reshape(tok_rows, route_count, experts)
    return (expert_float, slot_hot.reshape(tok_rows, route_count, capacity))


def expert_rows(rows, w_gate, w_up, w_down, groups=0):
    hidden_units = w_gate.shape[1]
    weights_in = lax.optimization_barrier(jnp.concatenate([w_gate, w_up], axis=1))
    parts = jnp.dot(rows, weights_in, preferred_element_type=jnp.float32)
    sent = parts.astype(jnp.bfloat16)
    others = [swapped(sent, same_mask(mask), False) for mask in range(GROUP - 1, 0, -1)]
    for other in others:
        parts = parts + other.astype(jnp.float32)
    inner_rows = (jax.nn.silu(parts[:, :hidden_units]) * parts[:, hidden_units:]).astype(
        jnp.bfloat16
    )
    partial_out = jnp.dot(inner_rows, w_down, preferred_element_type=jnp.float32)
    if not groups:
        return (partial_out + other_core(partial_out)).astype(jnp.bfloat16)
    own_rows = partial_out.shape[0] // groups
    near, far = partial_out[:own_rows], partial_out[own_rows:]
    near, far = lax.optimization_barrier((near, far))
    far_sum = (far + other_core(far)).astype(jnp.bfloat16)
    near_sum = (near + other_core(near)).astype(jnp.bfloat16)
    return near_sum, far_sum


def local(hidden, expert_ids, gate_scores, w_gate, w_up, w_down):
    tok_rows, width_all = hidden.shape
    route_count = expert_ids.shape[1]
    peer_count = lax.axis_size("ep")
    experts = peer_count // GROUP
    quarter = width_all // GROUP
    routing = (gate_scores / jnp.sum(gate_scores, axis=1, keepdims=True) * route_scale).astype(
        jnp.bfloat16
    )
    routing = routing.astype(jnp.float32)
    if route_count == experts:
        named = expert_ids[:, :, None] == jnp.arange(experts, dtype=jnp.int32)
        share = jnp.sum(jnp.where(named, routing[:, :, None], 0.0), axis=1)
        rows = spread_tokens(hidden).reshape(peer_count * tok_rows, quarter)
        near, far = expert_rows(rows, w_gate[0], w_up[0], w_down[0], experts)
        shares = [share[:, index : index + 1] for index in range(experts)]
        shares = by_xor(shares, lax.axis_index("ep") // GROUP)

        def weighted(block):
            total = sum(block[index].astype(jnp.float32) * shares[index] for index in range(experts))
            return total.astype(jnp.bfloat16)

        finished = return_tokens(
            near.reshape(-1, tok_rows, quarter), far.reshape(-1, tok_rows, quarter), weighted
        )
        return jnp.concatenate(finished, axis=1)
    capacity = min(tok_rows, 2 * tok_rows * route_count // experts)
    expert_hot, slot_hot = route_tables(expert_ids, experts, capacity)
    placing = jnp.einsum("tke,tkc->ect", expert_hot, slot_hot).astype(jnp.bfloat16)
    outgoing = jnp.einsum(
        "ect,tgd->egcd",
        placing,
        hidden.reshape(tok_rows, GROUP, quarter),
        preferred_element_type=jnp.float32,
    ).astype(jnp.bfloat16)
    outgoing = outgoing.reshape(peer_count, capacity, quarter)
    arrived = lax.all_to_all(outgoing, "ep", split_axis=0, concat_axis=0, tiled=True)
    rows = arrived.reshape(peer_count * capacity, quarter)
    expert_out = expert_rows(rows, w_gate[0], w_up[0], w_down[0])
    returned = lax.all_to_all(
        expert_out.reshape(peer_count, capacity, quarter),
        "ep",
        split_axis=0,
        concat_axis=0,
        tiled=True,
    ).reshape(experts, GROUP, capacity, quarter)
    combining = jnp.einsum("tk,tke,tkc->tec", routing, expert_hot, slot_hot).astype(jnp.bfloat16)
    combined = jnp.einsum(
        "tec,egcd->tgd", combining, returned, preferred_element_type=jnp.float32
    )
    return combined.reshape(tok_rows, width_all).astype(jnp.bfloat16)


def solution(mesh):
    return jax.shard_map(
        local,
        mesh=mesh,
        in_specs=(
            P(("groups", "ep"), None),
            P(("groups", "ep"), None),
            P(("groups", "ep"), None),
            P("ep", None, "tp"),
            P("ep", None, "tp"),
            P("ep", "tp", None),
        ),
        out_specs=P(("groups", "ep"), None),
        check_vma=False,
    )
```

```python
import jax
import jax.numpy as jnp
from jax import lax
from jax.sharding import PartitionSpec as P

GROUP = 4


route_scale = 2.5


def swapped(value, masks, crossed):
    ranks = lax.axis_size("ep")
    cores = lax.axis_size("tp")
    pairs = []
    for source in range(ranks):
        for core in range(cores):
            target_core = (core + 1) % cores if crossed else core
            pairs.append((source * cores + core, (source ^ masks[core]) * cores + target_core))
    return lax.ppermute(value, ("ep", "tp"), pairs)


def same_mask(mask):
    return [mask] * lax.axis_size("tp")


def other_core(value):
    return lax.ppermute(value, "tp", [(0, 1), (1, 0)])


def by_xor(blocks, rank):
    mask = 1
    while mask < len(blocks):
        bit = (rank & mask) > 0
        blocks = [
            jnp.where(bit, blocks[index ^ mask], blocks[index]) for index in range(len(blocks))
        ]
        mask *= 2
    return blocks


def quarters_of(rows):
    quarter = rows.shape[1] // GROUP
    return [rows[:, index * quarter : (index + 1) * quarter] for index in range(GROUP)]


def gathered(split, masks, crossed, shared, shared_crossed, arrive):
    third = masks[0] ^ masks[1]
    got = arrive(swapped(split, masks, crossed))
    both = arrive(swapped(shared, same_mask(third), shared_crossed))
    swap = other_core(got)
    swap, got, both = lax.optimization_barrier((swap, got, both))
    upper = lax.axis_index("tp") == 1
    lower_mask, upper_mask = reversed(masks) if crossed else masks
    return {
        third: both,
        lower_mask: jnp.where(upper, swap, got),
        upper_mask: jnp.where(upper, got, swap),
    }


def spread_tokens(hidden):
    rank = lax.axis_index("ep")

    def own_quarter(rows):
        return by_xor(quarters_of(rows), rank)[0]

    blocks = gathered(hidden, [3, 1], True, hidden, True, own_quarter)
    blocks[0] = lax.optimization_barrier(own_quarter(hidden))
    tokens = jnp.stack(by_xor([blocks[index] for index in range(GROUP)], rank))
    mask = GROUP
    while mask < lax.axis_size("ep"):
        tokens = jnp.concatenate([tokens, swapped(tokens, same_mask(mask), True)], axis=0)
        mask *= 2
    return tokens


def return_tokens(near, far):
    rank = lax.axis_index("ep")
    held = near[:, None]
    mask = GROUP
    if mask * 2 == lax.axis_size("ep"):
        other = swapped(far[:, None], same_mask(mask), True)
        other, held = lax.optimization_barrier((other, held))
        held = jnp.concatenate([held, other], axis=1)
        mask *= 2
    else:
        held = jnp.concatenate([near, far])[:, None]
    while mask < lax.axis_size("ep"):
        pairs = held.reshape((-1, 2, GROUP) + held.shape[1:])
        kept = pairs[:, 0].reshape((-1,) + held.shape[1:])
        sent = pairs[:, 1].reshape((-1,) + held.shape[1:])
        held = jnp.concatenate([kept, swapped(sent, same_mask(mask), True)], axis=1)
        mask *= 2
    leaving = by_xor([held[index] for index in range(GROUP)], rank)
    upper = lax.axis_index("tp") == 1
    masks = [1, 3]
    own, shared, split = lax.optimization_barrier(
        (leaving[0], leaving[2], jnp.where(upper, leaving[masks[1]], leaving[masks[0]]))
    )
    blocks = gathered(split, masks, False, shared, True, lambda block: block)
    blocks[0] = own
    return by_xor([blocks[index] for index in range(GROUP)], rank)


def route_tables(expert_ids, experts, capacity):
    tok_rows, route_count = expert_ids.shape
    flat_ids = expert_ids.reshape(-1)
    expert_hot = (flat_ids[:, None] == jnp.arange(experts, dtype=jnp.int32)[None, :]).astype(
        jnp.int32
    )
    ranking = jnp.sum((jnp.cumsum(expert_hot, axis=0) - expert_hot) * expert_hot, axis=1)
    slot_hot = (ranking[:, None] == jnp.arange(capacity, dtype=jnp.int32)[None, :]).astype(
        jnp.float32
    )
    expert_float = expert_hot.astype(jnp.float32).reshape(tok_rows, route_count, experts)
    return (expert_float, slot_hot.reshape(tok_rows, route_count, capacity))


def expert_rows(rows, w_gate, w_up, w_down, groups=0):
    hidden_units = w_gate.shape[1]
    weights_in = lax.optimization_barrier(jnp.concatenate([w_gate, w_up], axis=1))
    parts = jnp.dot(rows, weights_in, preferred_element_type=jnp.float32)
    sent = parts.astype(jnp.bfloat16)
    others = [swapped(sent, same_mask(mask), False) for mask in range(GROUP - 1, 0, -1)]
    for other in others:
        parts = parts + other.astype(jnp.float32)
    inner_rows = (jax.nn.silu(parts[:, :hidden_units]) * parts[:, hidden_units:]).astype(
        jnp.bfloat16
    )
    partial_out = jnp.dot(inner_rows, w_down, preferred_element_type=jnp.float32)
    if not groups:
        return (partial_out + other_core(partial_out)).astype(jnp.bfloat16)
    own_rows = partial_out.shape[0] // groups
    near, far = partial_out[:own_rows], partial_out[own_rows:]
    near, far = lax.optimization_barrier((near, far))
    far_sum = (far + other_core(far)).astype(jnp.bfloat16)
    near_sum = (near + other_core(near)).astype(jnp.bfloat16)
    return near_sum, far_sum


def local(hidden, expert_ids, gate_scores, w_gate, w_up, w_down):
    tok_rows, width_all = hidden.shape
    route_count = expert_ids.shape[1]
    peer_count = lax.axis_size("ep")
    experts = peer_count // GROUP
    quarter = width_all // GROUP
    routing = (gate_scores / jnp.sum(gate_scores, axis=1, keepdims=True) * route_scale).astype(
        jnp.bfloat16
    )
    routing = routing.astype(jnp.float32)
    if route_count == experts:
        named = expert_ids[:, :, None] == jnp.arange(experts, dtype=jnp.int32)
        share = jnp.sum(jnp.where(named, routing[:, :, None], 0.0), axis=1)
        rows = spread_tokens(hidden).reshape(peer_count * tok_rows, quarter)
        near, far = expert_rows(rows, w_gate[0], w_up[0], w_down[0], experts)
        returned = return_tokens(
            near.reshape(-1, tok_rows, quarter), far.reshape(-1, tok_rows, quarter)
        )
        shares = [share[:, index : index + 1] for index in range(experts)]
        shares = by_xor(shares, lax.axis_index("ep") // GROUP)
        combined = sum(
            jnp.concatenate([block[index] for block in returned], axis=1).astype(jnp.float32)
            * shares[index]
            for index in range(experts)
        )
        return combined.astype(jnp.bfloat16)
    capacity = min(tok_rows, 2 * tok_rows * route_count // experts)
    expert_hot, slot_hot = route_tables(expert_ids, experts, capacity)
    placing = jnp.einsum("tke,tkc->ect", expert_hot, slot_hot).astype(jnp.bfloat16)
    outgoing = jnp.einsum(
        "ect,tgd->egcd",
        placing,
        hidden.reshape(tok_rows, GROUP, quarter),
        preferred_element_type=jnp.float32,
    ).astype(jnp.bfloat16)
    outgoing = outgoing.reshape(peer_count, capacity, quarter)
    arrived = lax.all_to_all(outgoing, "ep", split_axis=0, concat_axis=0, tiled=True)
    rows = arrived.reshape(peer_count * capacity, quarter)
    expert_out = expert_rows(rows, w_gate[0], w_up[0], w_down[0])
    returned = lax.all_to_all(
        expert_out.reshape(peer_count, capacity, quarter),
        "ep",
        split_axis=0,
        concat_axis=0,
        tiled=True,
    ).reshape(experts, GROUP, capacity, quarter)
    combining = jnp.einsum("tk,tke,tkc->tec", routing, expert_hot, slot_hot).astype(jnp.bfloat16)
    combined = jnp.einsum(
        "tec,egcd->tgd", combining, returned, preferred_element_type=jnp.float32
    )
    return combined.reshape(tok_rows, width_all).astype(jnp.bfloat16)


def solution(mesh):
    return jax.shard_map(
        local,
        mesh=mesh,
        in_specs=(
            P(("groups", "ep"), None),
            P(("groups", "ep"), None),
            P(("groups", "ep"), None),
            P("ep", None, "tp"),
            P("ep", None, "tp"),
            P("ep", "tp", None),
        ),
        out_specs=P(("groups", "ep"), None),
        check_vma=False,
    )
```
